32 devices in a mesh: groups: 2 (over x), cells: 16 (over z, y, core).
Axes of the slice: x: 2, y: 2, z: 4, core: 2. Of those that a mesh axis runs over, the one named last changes fastest.
Arguments:
- snapshots: float32 [2176, 16384], P('cells', 'groups'), parts along dimension 1, may hold values from -6 to 6
- cell_volume: float32 [16384], P(('groups', 'cells')), parts along dimension 0, may hold values from 0.25 to 4
Outputs:
- modes: float32 [2, 128, 16, 16384], P(None, None, None, ('groups', 'cells')), parts along dimension 3
- upper_factor: float32 [4, 16, 16, 128], P('groups'), parts along dimension 0
The draws below stay inside these ranges and needn't reach their ends.
There are 2 independent parts, one for each index of `groups`. The reference program is written for one: setup_inputs(seed, part) draws one part's arguments, and reference() takes and returns one part's arrays. A program takes and returns all parts, laid end to end along the dimension named above; each array names one. Nothing has to cross between parts.
All inputs are finite; a program needn't handle non-finite values.
Results may differ from the reference program's by a relative error of at most 0.000073.
Values sent between devices are 32-bit elements; how exact they have to be, the bound alone decides.
A program may use at most 128 MiB of HBM per device.

```python
import math
import jax
import jax.numpy as jnp
from jax import lax

NFFT = 256
NF = 128
NB = 16
NT = 2176
CELLS = 8192


def level_of(rng, dims, split, low, high):
    def one(axis_at, shards_of):
        steps = jax.random.uniform(jax.random.fold_in(jax.random.fold_in(rng, 6), axis_at), (shards_of,), jnp.float32, low / len(split), high / len(split))
        return jnp.repeat(jnp.exp(steps), dims[axis_at] // shards_of).reshape((-1,) + (1,) * (len(dims) - axis_at - 1))

    factor_of = one(*split[0])
    for cut in split[1:]:
        factor_of = factor_of * one(*cut)
    return factor_of


def normal_values(own_key, extent, scale, bound, pieces=(), kind=jnp.bfloat16):
    result = scale * jax.random.normal(own_key, extent, jnp.float32)
    if pieces:
        result = result * level_of(own_key, extent, pieces, -0.22, 0.18)
    return jnp.clip(result, -bound, bound).astype(kind)


def setup_inputs(seed: int = 0, part: int = 0) -> dict:
    keys = jax.random.split(jax.random.key(seed), 3)
    part_splits = jax.random.split(jax.random.fold_in(keys[2], part), 3)
    snapshots = normal_values(part_splits[0], (NT, CELLS), 1.0, 6.0, ((0, 16),), jnp.float32)
    cell_volume = jnp.clip(jnp.exp(math.log(4.0) - 2.7725887 * jax.random.uniform(part_splits[1], (CELLS,), jnp.float32) ** level_of(part_splits[1], (CELLS,), ((0, 16),), -0.2, 0.2)), 0.25, 4.0)
    return dict(snapshots=snapshots, cell_volume=cell_volume)


def window_table(nfft, nfreq, nwin):
    steps = jnp.arange(nfft, dtype=jnp.int32)
    freqs = jnp.arange(nfreq, dtype=jnp.int32)
    tfloat = steps.astype(jnp.float32)
    window = 0.5 - 0.5 * jnp.cos(2.0 * jnp.pi * tfloat / nfft)
    scale = 1.0 / jnp.sqrt(nwin * jnp.sum(window * window))
    phase = (freqs[:, None] * steps[None, :] % nfft).astype(jnp.float32)
    angle = 2.0 * jnp.pi * phase / nfft
    cosine = window[None, :] * jnp.cos(angle) * scale
    sine = -window[None, :] * jnp.sin(angle) * scale
    return jnp.concatenate([cosine, sine], axis=0)

def cholesky_complex(gram_re, gram_im):
    count = gram_re.shape[0]
    places = jnp.arange(count, dtype=jnp.int32)
    cols_re = []
    cols_im = []
    for j in range(count):
        col_re = gram_re[:, j]
        col_im = gram_im[:, j]
        for k in range(j):
            piv_re = cols_re[k][j]
            piv_im = cols_im[k][j]
            col_re = col_re - (cols_re[k] * piv_re + cols_im[k] * piv_im)
            col_im = col_im - (cols_im[k] * piv_re - cols_re[k] * piv_im)
        pivot = jnp.sqrt(col_re[j])
        below = (places > j).astype(gram_re.dtype)[:, None]
        onto = (places == j).astype(gram_re.dtype)[:, None]
        cols_re.append(col_re / pivot * below + pivot * onto)
        cols_im.append(col_im / pivot * below)
    return (jnp.stack(cols_re, axis=1), jnp.stack(cols_im, axis=1))

def inverse_lower(low_re, low_im):
    count = low_re.shape[0]
    places = jnp.arange(count, dtype=jnp.int32)
    rows_re = []
    rows_im = []
    for i in range(count):
        unit = (places == i).astype(low_re.dtype)[:, None]
        row_re = unit + jnp.zeros_like(low_re[0])
        row_im = jnp.zeros_like(low_re[0])
        for k in range(i):
            part_re = low_re[i, k][None, :]
            part_im = low_im[i, k][None, :]
            row_re = row_re - (part_re * rows_re[k] - part_im * rows_im[k])
            row_im = row_im - (part_re * rows_im[k] + part_im * rows_re[k])
        diag = low_re[i, i][None, :]
        rows_re.append(row_re / diag)
        rows_im.append(row_im / diag)
    return (jnp.stack(rows_re, axis=0), jnp.stack(rows_im, axis=0))

def gram_of(amp_re, amp_im):
    high = lax.Precision.HIGHEST
    gram_re = jnp.einsum('jfc,kfc->jkf', amp_re, amp_re, precision=high) + jnp.einsum('jfc,kfc->jkf', amp_im, amp_im, precision=high)
    gram_im = jnp.einsum('jfc,kfc->jkf', amp_re, amp_im, precision=high) - jnp.einsum('jfc,kfc->jkf', amp_im, amp_re, precision=high)
    return (gram_re, gram_im)

def basis_of(inv_re, inv_im, amp_re, amp_im, weight):
    high = lax.Precision.HIGHEST
    basis_re = jnp.einsum('kjf,jfc->fkc', inv_re, amp_re, precision=high) + jnp.einsum('kjf,jfc->fkc', inv_im, amp_im, precision=high)
    basis_im = jnp.einsum('kjf,jfc->fkc', inv_re, amp_im, precision=high) - jnp.einsum('kjf,jfc->fkc', inv_im, amp_re, precision=high)
    return jnp.stack([basis_re, basis_im], axis=0) / weight

def reference(snapshots, cell_volume):
    centred = snapshots - lax.optimization_barrier(jnp.mean(snapshots, axis=0, keepdims=True))
    half = NFFT // 2
    halves = centred.reshape(NB + 1, half, CELLS)
    windows = jnp.concatenate([halves[:-1], halves[1:]], axis=1)
    table = window_table(NFFT, NF, NB)
    spectra = jnp.einsum('kt,btc->bkc', table, windows, precision=lax.Precision.HIGHEST).reshape(NB, 2, NF, CELLS)
    weight = jnp.sqrt(cell_volume / CELLS)
    amplitude = spectra * weight
    amp_re = amplitude[:, 0]
    amp_im = amplitude[:, 1]
    gram_re, gram_im = gram_of(amp_re, amp_im)
    low_re, low_im = cholesky_complex(gram_re, gram_im)
    inv_re, inv_im = inverse_lower(low_re, low_im)
    modes = basis_of(inv_re, inv_im, amp_re, amp_im, weight)
    upper_factor = jnp.stack([jnp.transpose(low_re, (1, 0, 2)), -jnp.transpose(low_im, (1, 0, 2))], axis=0)
    return (modes, upper_factor)
```

```python
import functools

import jax
import jax.numpy as jnp
import ml_dtypes
import numpy as np
from jax import lax
from jax.experimental import pallas as pl
from jax.experimental.pallas import tpu as pltpu
from jax.sharding import PartitionSpec as P

NFFT = 256
NF = 128
NB = 16
HALF = NFFT // 2
F8 = 8
GROUPS = NF // F8
BF16 = jnp.bfloat16
F32 = jnp.float32


def window_table():
    steps = np.arange(NFFT)
    freqs = np.arange(NF)
    window = 0.5 - 0.5 * np.cos(2.0 * np.pi * steps / NFFT)
    scale = 1.0 / np.sqrt(NB * np.sum(window * window))
    angle = 2.0 * np.pi * (freqs[:, None] * steps[None, :] % NFFT) / NFFT
    cosine = window[None, :] * np.cos(angle) * scale
    sine = -window[None, :] * np.sin(angle) * scale
    table = np.concatenate([cosine, sine], axis=0).astype(np.float32)
    high = table.astype(ml_dtypes.bfloat16)
    low = (table - high.astype(np.float32)).astype(ml_dtypes.bfloat16)
    return high, low


def split(value):
    high = value.astype(BF16)
    return high, (value - high.astype(F32)).astype(BF16)


def dot3(left, right, dims=(((1,), (0,)), ((), ()))):
    dot = functools.partial(lax.dot_general, dimension_numbers=dims, preferred_element_type=F32)
    return dot(left[0], right[0]) + (dot(left[0], right[1]) + dot(left[1], right[0]))


def same_frequency():
    sub = lax.broadcasted_iota(jnp.int32, (F8, NF), 0)
    lane = lax.broadcasted_iota(jnp.int32, (F8, NF), 1)
    return sub == lane % F8


def transform_chunk(first, load, centre, thi_ref, tlo_ref, w_ref, xhi, xlo, spec_ref, gram_ref, cols):
    for i in range(NB + 1):
        rows = slice(i * HALF, (i + 1) * HALF)
        xhi[rows], xlo[rows] = split(load(i) - centre)

    def one_window(b, _):
        rows = pl.ds(pl.multiple_of(b * HALF, HALF), NFFT)
        value = dot3((thi_ref[...], tlo_ref[...]), (xhi[rows], xlo[rows]))
        for ri in range(2):
            spec_ref[:, pl.ds(pl.multiple_of(ri * NF + b * F8, F8), F8), cols] = value[
                ri * NF : (ri + 1) * NF
            ].reshape(GROUPS, F8, -1)
        return 0

    lax.fori_loop(0, NB, one_window, 0, unroll=2)
    keep = same_frequency()[None]

    def one_group(g, _):
        parts = split(spec_ref[g, :, cols] * w_ref[:, cols])
        full = dot3(parts, parts, (((1,), (1,)), ((), ())))
        real = full[:NF, :NF] + full[NF:, NF:]
        imag = full[:NF, NF:] - full[NF:, :NF]
        for ri, value in enumerate((real, imag)):
            value = jnp.where(keep, value.reshape(NB, F8, NF), 0.0).sum(axis=1)
            gram_ref[ri, g] = value if first else gram_ref[ri, g] + value
        return 0

    lax.fori_loop(0, GROUPS, one_group, 0, unroll=2)


def transform_kernel(width, x_ref, w_ref, thi_ref, tlo_ref, spec_ref, gram_ref, xhi, xlo):
    cells = x_ref.shape[1]
    for at in range(0, cells, width):
        cols = slice(at, at + width)
        centre = jnp.mean(x_ref[:, cols], axis=0, keepdims=True)
        transform_chunk(
            at == 0, lambda i: x_ref[i * HALF : (i + 1) * HALF, cols], centre,
            thi_ref, tlo_ref, w_ref, xhi, xlo, spec_ref, gram_ref, cols,
        )


def transform(series, weight):
    slices, cells = series.shape
    width = min(cells, 256)
    vmem = pl.BlockSpec(memory_space=pltpu.VMEM)
    return pl.pallas_call(
        functools.partial(transform_kernel, width),
        out_shape=(
            jax.ShapeDtypeStruct((GROUPS, 2 * NF, cells), F32),
            jax.ShapeDtypeStruct((2, GROUPS, NB, NF), F32),
        ),
        in_specs=[vmem] * 4,
        out_specs=(vmem, vmem),
        scratch_shapes=[pltpu.VMEM((slices, width), BF16)] * 2,
        compiler_params=pltpu.CompilerParams(vmem_limit_bytes=48 * 2**20),
    )(series, weight, *window_table())


def factor(gram_re, gram_im):
    shape = gram_re.shape
    row = lax.broadcasted_iota(jnp.int32, shape, 1)
    lane = lax.broadcasted_iota(jnp.int32, shape, 2)
    block = lane // F8
    flat = (shape[0] * shape[1], shape[2])
    lane2 = lax.broadcasted_iota(jnp.int32, flat, 1)
    a_re, a_im = gram_re, gram_im
    w_re = (row == block).astype(F32)
    w_im = jnp.zeros(shape, F32)
    for j in range(NB):
        index = j * F8 + lane2 % F8

        def spread(value):
            return jnp.take_along_axis(
                value.reshape(flat), index, axis=1, mode="promise_in_bounds"
            ).reshape(shape)

        c_re, c_im = spread(a_re), spread(a_im)
        inverse = 1.0 / jnp.sqrt(c_re[:, j : j + 1])
        l_re = jnp.where(row > j, c_re * inverse, 0.0)
        l_im = jnp.where(row > j, c_im * inverse, 0.0)

        def eliminate(v_re, v_im):
            p_re, p_im = v_re[:, j : j + 1] * inverse, v_im[:, j : j + 1] * inverse
            return (
                jnp.where(row == j, p_re, v_re - (l_re * p_re - l_im * p_im)),
                jnp.where(row == j, p_im, v_im - (l_re * p_im + l_im * p_re)),
            )

        a_re, a_im = eliminate(a_re, a_im)
        w_re, w_im = eliminate(w_re, w_im)
    a_re = jnp.where(block >= row, a_re, 0.0)
    a_im = jnp.where(block > row, a_im, 0.0)
    return a_re, a_im, w_re, w_im


def modes_kernel(gram_ref, spec_ref, modes_ref, upper_ref, inv):
    @pl.when(pl.program_id(0) == 0)
    def _():
        upper_ref[0], upper_ref[1], inv[0], inv[1] = factor(gram_ref[0], gram_ref[1])

    g = pl.program_id(0)
    sub = lax.broadcasted_iota(jnp.int32, (F8, NB, NF), 0)
    lane = lax.broadcasted_iota(jnp.int32, (F8, NB, NF), 2)
    keep = sub == lane % F8
    real, imag = [
        jnp.where(keep, jnp.broadcast_to(inv[ri, g][None], keep.shape), 0.0).reshape(NF, NF)
        for ri in range(2)
    ]
    matrix = jnp.concatenate(
        [jnp.concatenate([real, imag], axis=1), jnp.concatenate([-imag, real], axis=1)], axis=0
    )
    value = dot3(split(matrix), split(spec_ref[0]))
    modes_ref[...] = value.reshape(2, F8, NB, -1)


def finish(gram, spec):
    cells = spec.shape[2]
    whole = (2, GROUPS, NB, NF)
    return pl.pallas_call(
        modes_kernel,
        grid=(GROUPS,),
        out_shape=(
            jax.ShapeDtypeStruct((2, NF, NB, cells), F32),
            jax.ShapeDtypeStruct(whole, F32),
        ),
        in_specs=[
            pl.BlockSpec(whole, lambda g: (0, 0, 0, 0)),
            pl.BlockSpec((1, 2 * NF, cells), lambda g: (g, 0, 0)),
        ],
        out_specs=(
            pl.BlockSpec((2, F8, NB, cells), lambda g: (0, g, 0, 0)),
            pl.BlockSpec(whole, lambda g: (0, 0, 0, 0)),
        ),
        scratch_shapes=[pltpu.VMEM(whole, F32)],
        compiler_params=pltpu.CompilerParams(vmem_limit_bytes=32 * 2**20),
    )(gram, spec)


def on_device(snapshots, cell_volume):
    cells = cell_volume.shape[0]
    slices = snapshots.shape[0]
    members = lax.axis_size("cells")
    weight = jnp.sqrt(cell_volume / (cells * members))[None]
    blocks = snapshots.reshape(slices, members, cells)
    series = lax.all_to_all(blocks, "cells", split_axis=1, concat_axis=0, tiled=True)[:, 0, :]
    spec, gram = transform(series, weight)
    gram = lax.psum(gram, "cells")
    modes, upper = finish(gram, spec)
    upper = upper.reshape(2, GROUPS, NB, NB, F8).transpose(0, 2, 3, 1, 4).reshape(2, NB, NB, NF)
    return modes, upper


def solution(mesh):
    return jax.shard_map(
        on_device,
        mesh=mesh,
        in_specs=(P("cells", "groups"), P(("groups", "cells"))),
        out_specs=(P(None, None, None, ("groups", "cells")), P("groups", None, None, None)),
        check_vma=False,
    )
```

```python
import functools

import jax
import jax.numpy as jnp
import ml_dtypes
import numpy as np
from jax import lax
from jax.experimental import pallas as pl
from jax.experimental.pallas import tpu as pltpu
from jax.sharding import PartitionSpec as P

NFFT = 256
NF = 128
NB = 16
HALF = NFFT // 2
F8 = 8
GROUPS = NF // F8
BF16 = jnp.bfloat16
F32 = jnp.float32


def window_table():
    steps = np.arange(NFFT)
    freqs = np.arange(NF)
    window = 0.5 - 0.5 * np.cos(2.0 * np.pi * steps / NFFT)
    scale = 1.0 / np.sqrt(NB * np.sum(window * window))
    angle = 2.0 * np.pi * (freqs[:, None] * steps[None, :] % NFFT) / NFFT
    cosine = window[None, :] * np.cos(angle) * scale
    sine = -window[None, :] * np.sin(angle) * scale
    table = np.concatenate([cosine, sine], axis=0).astype(np.float32)
    high = table.astype(ml_dtypes.bfloat16)
    low = (table - high.astype(np.float32)).astype(ml_dtypes.bfloat16)
    return high, low


def split(value):
    high = value.astype(BF16)
    return high, (value - high.astype(F32)).astype(BF16)


def dot3(left, right, dims=(((1,), (0,)), ((), ()))):
    dot = functools.partial(lax.dot_general, dimension_numbers=dims, preferred_element_type=F32)
    return dot(left[0], right[0]) + (dot(left[0], right[1]) + dot(left[1], right[0]))


def same_frequency():
    sub = lax.broadcasted_iota(jnp.int32, (F8, NF), 0)
    lane = lax.broadcasted_iota(jnp.int32, (F8, NF), 1)
    return sub == lane % F8


def transform_chunk(first, load, centre, thi_ref, tlo_ref, w_ref, xhi, xlo, spec_ref, gram_ref, cols):
    for i in range(NB + 1):
        rows = slice(i * HALF, (i + 1) * HALF)
        xhi[rows], xlo[rows] = split(load(i) - centre)

    def one_window(b, _):
        rows = pl.ds(pl.multiple_of(b * HALF, HALF), NFFT)
        value = dot3((thi_ref[...], tlo_ref[...]), (xhi[rows], xlo[rows]))
        for ri in range(2):
            spec_ref[:, pl.ds(pl.multiple_of(ri * NF + b * F8, F8), F8), cols] = value[
                ri * NF : (ri + 1) * NF
            ].reshape(GROUPS, F8, -1)
        return 0

    lax.fori_loop(0, NB, one_window, 0, unroll=2)
    keep = same_frequency()[None]

    def one_group(g, _):
        parts = split(spec_ref[g, :, cols] * w_ref[:, cols])
        full = dot3(parts, parts, (((1,), (1,)), ((), ())))
        real = full[:NF, :NF] + full[NF:, NF:]
        imag = full[:NF, NF:] - full[NF:, :NF]
        for ri, value in enumerate((real, imag)):
            value = jnp.where(keep, value.reshape(NB, F8, NF), 0.0).sum(axis=1)
            gram_ref[ri, g] = value if first else gram_ref[ri, g] + value
        return 0

    lax.fori_loop(0, GROUPS, one_group, 0, unroll=2)


def transform_kernel(width, x_ref, w_ref, thi_ref, tlo_ref, spec_ref, gram_ref, xhi, xlo):
    cells = x_ref.shape[1]
    for at in range(0, cells, width):
        cols = slice(at, at + width)
        centre = jnp.mean(x_ref[:, cols], axis=0, keepdims=True)
        transform_chunk(
            at == 0, lambda i: x_ref[i * HALF : (i + 1) * HALF, cols], centre,
            thi_ref, tlo_ref, w_ref, xhi, xlo, spec_ref, gram_ref, cols,
        )


def transform(series, weight):
    slices, cells = series.shape
    width = min(cells, 256)
    vmem = pl.BlockSpec(memory_space=pltpu.VMEM)
    return pl.pallas_call(
        functools.partial(transform_kernel, width),
        out_shape=(
            jax.ShapeDtypeStruct((GROUPS, 2 * NF, cells), F32),
            jax.ShapeDtypeStruct((2, GROUPS, NB, NF), F32),
        ),
        in_specs=[vmem] * 4,
        out_specs=(vmem, vmem),
        scratch_shapes=[pltpu.VMEM((slices, width), BF16)] * 2,
        compiler_params=pltpu.CompilerParams(vmem_limit_bytes=48 * 2**20),
    )(series, weight, *window_table())


def peer(members, off):
    return {"cells": lax.rem(lax.axis_index("cells") + off, members)}


def greet(members):
    barrier = pltpu.get_barrier_semaphore()

    def one(off, _):
        pl.semaphore_signal(
            barrier, inc=1, device_id=peer(members, off), device_id_type=pl.DeviceIdType.MESH
        )
        return 0

    lax.fori_loop(1, members, one, 0)
    pl.semaphore_wait(barrier, members - 1)


def all_sum(members, part_ref, land, gather, sems):
    me = lax.axis_index("cells")

    def share(off):
        return pltpu.make_async_remote_copy(
            src_ref=part_ref.at[lax.rem(me + off, members)],
            dst_ref=land.at[off],
            send_sem=sems.at[0, off],
            recv_sem=sems.at[1, off],
            device_id=peer(members, off),
            device_id_type=pl.DeviceIdType.MESH,
        )

    def result(off):
        return pltpu.make_async_remote_copy(
            src_ref=gather.at[me],
            dst_ref=gather.at[me],
            send_sem=sems.at[2, off],
            recv_sem=sems.at[3, off],
            device_id=peer(members, off),
            device_id_type=pl.DeviceIdType.MESH,
        )

    def loop(body):
        def one(off, _):
            body(off)
            return 0

        lax.fori_loop(1, members, one, 0)

    loop(lambda off: share(off).start())
    land[0] = part_ref[me]
    loop(lambda off: share(off).wait())
    gather[me] = jnp.sum(land[...], axis=0)
    loop(lambda off: result(off).start())
    loop(lambda off: result(off).wait())


def sum_kernel(members, part_ref, out_ref, land, gather, sems):
    greet(members)
    all_sum(members, part_ref, land, gather, sems)
    out_ref[...] = gather[...]


def sum_over_cells(gram, members):
    parts = gram.reshape(members, -1, NF)
    vmem = pl.BlockSpec(memory_space=pltpu.VMEM)
    return pl.pallas_call(
        functools.partial(sum_kernel, members),
        out_shape=jax.ShapeDtypeStruct(parts.shape, F32),
        in_specs=[vmem],
        out_specs=vmem,
        scratch_shapes=[
            pltpu.VMEM(parts.shape, F32),
            pltpu.VMEM(parts.shape, F32),
            pltpu.SemaphoreType.DMA((4, members)),
        ],
        compiler_params=pltpu.CompilerParams(collective_id=0, has_side_effects=True),
    )(parts).reshape(gram.shape)


def factor(gram_re, gram_im):
    shape = gram_re.shape
    row = lax.broadcasted_iota(jnp.int32, shape, 1)
    lane = lax.broadcasted_iota(jnp.int32, shape, 2)
    block = lane // F8
    flat = (shape[0] * shape[1], shape[2])
    lane2 = lax.broadcasted_iota(jnp.int32, flat, 1)
    a_re, a_im = gram_re, gram_im
    w_re = (row == block).astype(F32)
    w_im = jnp.zeros(shape, F32)
    for j in range(NB):
        index = j * F8 + lane2 % F8

        def spread(value):
            return jnp.take_along_axis(
                value.reshape(flat), index, axis=1, mode="promise_in_bounds"
            ).reshape(shape)

        c_re, c_im = spread(a_re), spread(a_im)
        inverse = 1.0 / jnp.sqrt(c_re[:, j : j + 1])
        l_re = jnp.where(row > j, c_re * inverse, 0.0)
        l_im = jnp.where(row > j, c_im * inverse, 0.0)

        def eliminate(v_re, v_im):
            p_re, p_im = v_re[:, j : j + 1] * inverse, v_im[:, j : j + 1] * inverse
            return (
                jnp.where(row == j, p_re, v_re - (l_re * p_re - l_im * p_im)),
                jnp.where(row == j, p_im, v_im - (l_re * p_im + l_im * p_re)),
            )

        a_re, a_im = eliminate(a_re, a_im)
        w_re, w_im = eliminate(w_re, w_im)
    a_re = jnp.where(block >= row, a_re, 0.0)
    a_im = jnp.where(block > row, a_im, 0.0)
    return a_re, a_im, w_re, w_im


def modes_kernel(gram_ref, spec_ref, modes_ref, upper_ref, inv):
    @pl.when(pl.program_id(0) == 0)
    def _():
        upper_ref[0], upper_ref[1], inv[0], inv[1] = factor(gram_ref[0], gram_ref[1])

    g = pl.program_id(0)
    sub = lax.broadcasted_iota(jnp.int32, (F8, NB, NF), 0)
    lane = lax.broadcasted_iota(jnp.int32, (F8, NB, NF), 2)
    keep = sub == lane % F8
    real, imag = [
        jnp.where(keep, jnp.broadcast_to(inv[ri, g][None], keep.shape), 0.0).reshape(NF, NF)
        for ri in range(2)
    ]
    matrix = jnp.concatenate(
        [jnp.concatenate([real, imag], axis=1), jnp.concatenate([-imag, real], axis=1)], axis=0
    )
    value = dot3(split(matrix), split(spec_ref[0]))
    modes_ref[...] = value.reshape(2, F8, NB, -1)


def finish(gram, spec):
    cells = spec.shape[2]
    whole = (2, GROUPS, NB, NF)
    return pl.pallas_call(
        modes_kernel,
        grid=(GROUPS,),
        out_shape=(
            jax.ShapeDtypeStruct((2, NF, NB, cells), F32),
            jax.ShapeDtypeStruct(whole, F32),
        ),
        in_specs=[
            pl.BlockSpec(whole, lambda g: (0, 0, 0, 0)),
            pl.BlockSpec((1, 2 * NF, cells), lambda g: (g, 0, 0)),
        ],
        out_specs=(
            pl.BlockSpec((2, F8, NB, cells), lambda g: (0, g, 0, 0)),
            pl.BlockSpec(whole, lambda g: (0, 0, 0, 0)),
        ),
        scratch_shapes=[pltpu.VMEM(whole, F32)],
        compiler_params=pltpu.CompilerParams(vmem_limit_bytes=32 * 2**20),
    )(gram, spec)


def on_device(snapshots, cell_volume):
    cells = cell_volume.shape[0]
    slices = snapshots.shape[0]
    members = lax.axis_size("cells")
    weight = jnp.sqrt(cell_volume / (cells * members))[None]
    blocks = snapshots.reshape(slices, members, cells)
    series = lax.all_to_all(blocks, "cells", split_axis=1, concat_axis=0, tiled=True)[:, 0, :]
    spec, gram = transform(series, weight)
    gram = sum_over_cells(gram, members)
    modes, upper = finish(gram, spec)
    upper = upper.reshape(2, GROUPS, NB, NB, F8).transpose(0, 2, 3, 1, 4).reshape(2, NB, NB, NF)
    return modes, upper


def solution(mesh):
    return jax.shard_map(
        on_device,
        mesh=mesh,
        in_specs=(P("cells", "groups"), P(("groups", "cells"))),
        out_specs=(P(None, None, None, ("groups", "cells")), P("groups", None, None, None)),
        check_vma=False,
    )
```

```python
import functools

import jax
import jax.numpy as jnp
import ml_dtypes
import numpy as np
from jax import lax
from jax.experimental import pallas as pl
from jax.experimental.pallas import tpu as pltpu
from jax.sharding import PartitionSpec as P

NFFT = 256
NF = 128
NB = 16
HALF = NFFT // 2
F8 = 8
GROUPS = NF // F8
WIDTH = 256
BF16 = jnp.bfloat16
F32 = jnp.float32


def window_table():
    steps = np.arange(NFFT)
    freqs = np.arange(NF)
    window = 0.5 - 0.5 * np.cos(2.0 * np.pi * steps / NFFT)
    scale = 1.0 / np.sqrt(NB * np.sum(window * window))
    angle = 2.0 * np.pi * (freqs[:, None] * steps[None, :] % NFFT) / NFFT
    cosine = window[None, :] * np.cos(angle) * scale
    sine = -window[None, :] * np.sin(angle) * scale
    table = np.concatenate([cosine, sine], axis=0).astype(np.float32)
    high = table.astype(ml_dtypes.bfloat16)
    low = (table - high.astype(np.float32)).astype(ml_dtypes.bfloat16)
    return high, low


def split(value):
    high = value.astype(BF16)
    return high, (value - high.astype(F32)).astype(BF16)


def dot3(left, right, dims=(((1,), (0,)), ((), ()))):
    dot = functools.partial(lax.dot_general, dimension_numbers=dims, preferred_element_type=F32)
    return dot(left[0], right[0]) + (dot(left[0], right[1]) + dot(left[1], right[0]))


def same_frequency():
    sub = lax.broadcasted_iota(jnp.int32, (F8, NF), 0)
    lane = lax.broadcasted_iota(jnp.int32, (F8, NF), 1)
    return sub == lane % F8


def transform_chunk(first, load, centre, thi_ref, tlo_ref, w_ref, xhi, xlo, spec_ref, gram_ref, cols):
    for i in range(NB + 1):
        rows = slice(i * HALF, (i + 1) * HALF)
        xhi[rows], xlo[rows] = split(load(i) - centre)

    def one_window(b, _):
        rows = pl.ds(pl.multiple_of(b * HALF, HALF), NFFT)
        value = dot3((thi_ref[...], tlo_ref[...]), (xhi[rows], xlo[rows]))
        for ri in range(2):
            spec_ref[:, pl.ds(pl.multiple_of(ri * NF + b * F8, F8), F8), cols] = value[
                ri * NF : (ri + 1) * NF
            ].reshape(GROUPS, F8, -1)
        return 0

    lax.fori_loop(0, NB, one_window, 0, unroll=2)
    keep = same_frequency()[None]

    def one_group(g, _):
        parts = split(spec_ref[g, :, cols] * w_ref[:, cols])
        full = dot3(parts, parts, (((1,), (1,)), ((), ())))
        real = full[:NF, :NF] + full[NF:, NF:]
        imag = full[:NF, NF:] - full[NF:, :NF]
        for ri, value in enumerate((real, imag)):
            value = jnp.where(keep, value.reshape(NB, F8, NF), 0.0).sum(axis=1)
            rows = pl.ds(pl.multiple_of((ri * GROUPS + g) * NB, NB), NB)
            gram_ref[rows] = value if first else gram_ref[rows] + value
        return 0

    lax.fori_loop(0, GROUPS, one_group, 0, unroll=2)


def transform_kernel(width, x_ref, w_ref, thi_ref, tlo_ref, spec_ref, gram_ref, xhi, xlo):
    cells = x_ref.shape[1]
    for at in range(0, cells, width):
        cols = slice(at, at + width)
        centre = jnp.mean(x_ref[:, cols], axis=0, keepdims=True)
        transform_chunk(
            at == 0, lambda i: x_ref[i * HALF : (i + 1) * HALF, cols], centre,
            thi_ref, tlo_ref, w_ref, xhi, xlo, spec_ref, gram_ref, cols,
        )


def transform(series, weight):
    slices, cells = series.shape
    width = min(cells, 256)
    vmem = pl.BlockSpec(memory_space=pltpu.VMEM)
    return pl.pallas_call(
        functools.partial(transform_kernel, width),
        out_shape=(
            jax.ShapeDtypeStruct((GROUPS, 2 * NF, cells), F32),
            jax.ShapeDtypeStruct((2 * GROUPS * NB, NF), F32),
        ),
        in_specs=[vmem] * 4,
        out_specs=(vmem, vmem),
        scratch_shapes=[pltpu.VMEM((slices, width), BF16)] * 2,
        compiler_params=pltpu.CompilerParams(vmem_limit_bytes=48 * 2**20),
    )(series, weight, *window_table())


def peer(members, off):
    return {"cells": lax.rem(lax.axis_index("cells") + off, members)}


def greet(members):
    barrier = pltpu.get_barrier_semaphore()

    def one(off, _):
        pl.semaphore_signal(
            barrier, inc=1, device_id=peer(members, off), device_id_type=pl.DeviceIdType.MESH
        )
        return 0

    lax.fori_loop(1, members, one, 0)
    pl.semaphore_wait(barrier, members - 1)


def all_sum(members, part_ref, land, gather, sems):
    me = lax.axis_index("cells")
    rows = part_ref.shape[0] // members

    def of(member):
        return pl.ds(pl.multiple_of(member * rows, rows), rows)

    def share(off):
        return pltpu.make_async_remote_copy(
            src_ref=part_ref.at[of(lax.rem(me + off, members))],
            dst_ref=land.at[off],
            send_sem=sems.at[0, off],
            recv_sem=sems.at[1, off],
            device_id=peer(members, off),
            device_id_type=pl.DeviceIdType.MESH,
        )

    def result(off):
        return pltpu.make_async_remote_copy(
            src_ref=gather.at[of(me)],
            dst_ref=gather.at[of(me)],
            send_sem=sems.at[2, off],
            recv_sem=sems.at[3, off],
            device_id=peer(members, off),
            device_id_type=pl.DeviceIdType.MESH,
        )

    def loop(body):
        def one(off, _):
            body(off)
            return 0

        lax.fori_loop(1, members, one, 0)

    loop(lambda off: share(off).start())
    land[0] = part_ref[of(me)]
    loop(lambda off: share(off).wait())
    gather[of(me)] = jnp.sum(land[...], axis=0)
    loop(lambda off: result(off).start())
    loop(lambda off: result(off).wait())


def sum_kernel(members, part_ref, out_ref, land, gather, sems):
    greet(members)
    all_sum(members, part_ref, land, gather, sems)
    out_ref[...] = gather[...]


def sum_over_cells(gram, members):
    vmem = pl.BlockSpec(memory_space=pltpu.VMEM)
    return pl.pallas_call(
        functools.partial(sum_kernel, members),
        out_shape=jax.ShapeDtypeStruct(gram.shape, F32),
        in_specs=[vmem],
        out_specs=vmem,
        scratch_shapes=[
            pltpu.VMEM((members, gram.shape[0] // members, NF), F32),
            pltpu.VMEM(gram.shape, F32),
            pltpu.SemaphoreType.DMA((4, members)),
        ],
        compiler_params=pltpu.CompilerParams(collective_id=0, has_side_effects=True),
    )(gram)


def exchange_kernel(
    members, width, x_ref, w_ref, thi_ref, tlo_ref, spec_out, gram_out,
    arrived, spec, xhi, xlo, gram, land, gather, own_sem, send_sem, recv_sem, out_sem, sum_sem,
):
    me = lax.axis_index("cells")
    slices = x_ref.shape[0]
    cells = x_ref.shape[1] // members
    chunks = cells // width
    mine = pl.ds(pl.multiple_of(me * slices, 8), slices)

    def source(member, chunk):
        return x_ref.at[:, pl.ds(pl.multiple_of(member * cells + chunk * width, width), width)]

    def own(chunk):
        return pltpu.make_async_copy(
            source(me, chunk), arrived.at[chunk, mine], own_sem.at[chunk]
        )

    def remote(chunk, off):
        return pltpu.make_async_remote_copy(
            src_ref=source(lax.rem(me + off, members), chunk),
            dst_ref=arrived.at[chunk, mine],
            send_sem=send_sem.at[chunk, off],
            recv_sem=recv_sem.at[chunk, off],
            device_id=peer(members, off),
            device_id_type=pl.DeviceIdType.MESH,
        )

    def store(chunk):
        cols = slice(chunk * width, (chunk + 1) * width)
        return pltpu.make_async_copy(
            spec.at[:, :, cols], spec_out.at[:, :, cols], out_sem.at[chunk]
        )

    def loop(body):
        def one(off, _):
            body(off)
            return 0

        lax.fori_loop(1, members, one, 0)

    for chunk in range(chunks):
        own(chunk).start()
    greet(members)
    for chunk in range(chunks):
        for off in sorted(range(1, members), key=lambda off: abs(off - members // 2)):
            remote(chunk, off).start()
    for chunk in range(chunks):
        own(chunk).wait()
        loop(lambda off: remote(chunk, off).wait_recv())
        cols = slice(chunk * width, (chunk + 1) * width)
        centre = jnp.mean(arrived[chunk], axis=0, keepdims=True)
        transform_chunk(
            chunk == 0, lambda i: arrived[chunk, i * HALF : (i + 1) * HALF], centre,
            thi_ref, tlo_ref, w_ref, xhi, xlo, spec, gram, cols,
        )
        store(chunk).start()
    all_sum(members, gram, land, gather, sum_sem)
    gram_out[...] = gather[...]
    for chunk in range(chunks):
        loop(lambda off: remote(chunk, off).wait_send())
        store(chunk).wait()


def exchange(snapshots, weight, members):
    slices = snapshots.shape[0]
    cells = weight.shape[1]
    width = min(cells, WIDTH)
    chunks = cells // width
    total = slices * members
    spec = (GROUPS, 2 * NF, cells)
    gram = (2 * GROUPS * NB, NF)
    vmem = pl.BlockSpec(memory_space=pltpu.VMEM)
    anywhere = pl.BlockSpec(memory_space=pl.ANY)
    return pl.pallas_call(
        functools.partial(exchange_kernel, members, width),
        out_shape=(jax.ShapeDtypeStruct(spec, F32), jax.ShapeDtypeStruct(gram, F32)),
        in_specs=[anywhere, vmem, vmem, vmem],
        out_specs=(anywhere, vmem),
        scratch_shapes=[
            pltpu.VMEM((chunks, total, width), F32),
            pltpu.VMEM(spec, F32),
            pltpu.VMEM((total, width), BF16),
            pltpu.VMEM((total, width), BF16),
            pltpu.VMEM(gram, F32),
            pltpu.VMEM((members, gram[0] // members, NF), F32),
            pltpu.VMEM(gram, F32),
            pltpu.SemaphoreType.DMA((chunks,)),
            pltpu.SemaphoreType.DMA((chunks, members)),
            pltpu.SemaphoreType.DMA((chunks, members)),
            pltpu.SemaphoreType.DMA((chunks,)),
            pltpu.SemaphoreType.DMA((4, members)),
        ],
        compiler_params=pltpu.CompilerParams(
            collective_id=1, has_side_effects=True, vmem_limit_bytes=48 * 2**20
        ),
    )(snapshots, weight, *window_table())


def factor(gram_re, gram_im):
    shape = gram_re.shape
    row = lax.broadcasted_iota(jnp.int32, shape, 1)
    lane = lax.broadcasted_iota(jnp.int32, shape, 2)
    block = lane // F8
    flat = (shape[0] * shape[1], shape[2])
    lane2 = lax.broadcasted_iota(jnp.int32, flat, 1)
    a_re, a_im = gram_re, gram_im
    w_re = (row == block).astype(F32)
    w_im = jnp.zeros(shape, F32)
    for j in range(NB):
        index = j * F8 + lane2 % F8

        def spread(value):
            return jnp.take_along_axis(
                value.reshape(flat), index, axis=1, mode="promise_in_bounds"
            ).reshape(shape)

        c_re, c_im = spread(a_re), spread(a_im)
        inverse = 1.0 / jnp.sqrt(c_re[:, j : j + 1])
        l_re = jnp.where(row > j, c_re * inverse, 0.0)
        l_im = jnp.where(row > j, c_im * inverse, 0.0)

        def eliminate(v_re, v_im):
            p_re, p_im = v_re[:, j : j + 1] * inverse, v_im[:, j : j + 1] * inverse
            return (
                jnp.where(row == j, p_re, v_re - (l_re * p_re - l_im * p_im)),
                jnp.where(row == j, p_im, v_im - (l_re * p_im + l_im * p_re)),
            )

        a_re, a_im = eliminate(a_re, a_im)
        w_re, w_im = eliminate(w_re, w_im)
    a_re = jnp.where(block >= row, a_re, 0.0)
    a_im = jnp.where(block > row, a_im, 0.0)
    return a_re, a_im, w_re, w_im


def by_frequency(upper, out_ref, ri):
    block = lax.broadcasted_iota(jnp.int32, (NB, NF), 1) // F8
    turned = [pltpu.roll(upper[g], g * F8, 1) if g else upper[g] for g in range(GROUPS)]
    for k in range(NB):
        value = turned[0]
        for g in range(1, GROUPS):
            value = jnp.where(block == (g + k) % NB, turned[g], value)
        out_ref[ri, :, k, :] = pltpu.roll(value, (NF - k * F8) % NF, 1) if k else value


def modes_kernel(gram_ref, spec_ref, modes_ref, upper_ref, inv):
    @pl.when(pl.program_id(0) == 0)
    def _():
        upper_re, upper_im, inv[0], inv[1] = factor(gram_ref[0], gram_ref[1])
        for ri, upper in enumerate((upper_re, upper_im)):
            by_frequency(upper, upper_ref, ri)

    g = pl.program_id(0)
    sub = lax.broadcasted_iota(jnp.int32, (F8, NB, NF), 0)
    lane = lax.broadcasted_iota(jnp.int32, (F8, NB, NF), 2)
    keep = sub == lane % F8
    real, imag = [
        jnp.where(keep, jnp.broadcast_to(inv[ri, g][None], keep.shape), 0.0).reshape(NF, NF)
        for ri in range(2)
    ]
    matrix = jnp.concatenate(
        [jnp.concatenate([real, imag], axis=1), jnp.concatenate([-imag, real], axis=1)], axis=0
    )
    value = dot3(split(matrix), split(spec_ref[0]))
    modes_ref[...] = value.reshape(2, F8, NB, -1)


def finish(gram, spec):
    cells = spec.shape[2]
    whole = (2, GROUPS, NB, NF)
    return pl.pallas_call(
        modes_kernel,
        grid=(GROUPS,),
        out_shape=(
            jax.ShapeDtypeStruct((2, NF, NB, cells), F32),
            jax.ShapeDtypeStruct((2, NB, NB, NF), F32),
        ),
        in_specs=[
            pl.BlockSpec(whole, lambda g: (0, 0, 0, 0)),
            pl.BlockSpec((1, 2 * NF, cells), lambda g: (g, 0, 0)),
        ],
        out_specs=(
            pl.BlockSpec((2, F8, NB, cells), lambda g: (0, g, 0, 0)),
            pl.BlockSpec((2, NB, NB, NF), lambda g: (0, 0, 0, 0)),
        ),
        scratch_shapes=[pltpu.VMEM(whole, F32)],
        compiler_params=pltpu.CompilerParams(vmem_limit_bytes=32 * 2**20),
    )(gram, spec)


def on_device(snapshots, cell_volume):
    cells = cell_volume.shape[0]
    slices = snapshots.shape[0]
    members = lax.axis_size("cells")
    weight = jnp.sqrt(cell_volume / (cells * members))[None]
    if slices % 8 == 0 and cells % WIDTH == 0:
        spec, gram = exchange(snapshots, weight, members)
    else:
        blocks = snapshots.reshape(slices, members, cells)
        series = lax.all_to_all(blocks, "cells", split_axis=1, concat_axis=0, tiled=True)[:, 0, :]
        spec, gram = transform(series, weight)
        gram = sum_over_cells(gram, members)
    return finish(gram.reshape(2, GROUPS, NB, NF), spec)


def solution(mesh):
    return jax.shard_map(
        on_device,
        mesh=mesh,
        in_specs=(P("cells", "groups"), P(("groups", "cells"))),
        out_specs=(P(None, None, None, ("groups", "cells")), P("groups", None, None, None)),
        check_vma=False,
    )
```

```python
import functools

import jax
import jax.numpy as jnp
import ml_dtypes
import numpy as np
from jax import lax
from jax.experimental import pallas as pl
from jax.experimental.pallas import tpu as pltpu
from jax.sharding import PartitionSpec as P

NFFT = 256
NF = 128
NB = 16
HALF = NFFT // 2
F8 = 8
GROUPS = NF // F8
WIDTH = 128
BF16 = jnp.bfloat16
F32 = jnp.float32


def window_table():
    steps = np.arange(NFFT)
    freqs = np.arange(NF)
    window = 0.5 - 0.5 * np.cos(2.0 * np.pi * steps / NFFT)
    scale = 1.0 / np.sqrt(NB * np.sum(window * window))
    angle = 2.0 * np.pi * (freqs[:, None] * steps[None, :] % NFFT) / NFFT
    cosine = window[None, :] * np.cos(angle) * scale
    sine = -window[None, :] * np.sin(angle) * scale
    table = np.concatenate([cosine, sine], axis=0).astype(np.float32)
    high = table.astype(ml_dtypes.bfloat16)
    low = (table - high.astype(np.float32)).astype(ml_dtypes.bfloat16)
    return high, low


def split(value):
    high = value.astype(BF16)
    return high, (value - high.astype(F32)).astype(BF16)


def dot3(left, right, dims=(((1,), (0,)), ((), ()))):
    dot = functools.partial(lax.dot_general, dimension_numbers=dims, preferred_element_type=F32)
    return dot(left[0], right[0]) + (dot(left[0], right[1]) + dot(left[1], right[0]))


def same_frequency():
    sub = lax.broadcasted_iota(jnp.int32, (F8, NF), 0)
    lane = lax.broadcasted_iota(jnp.int32, (F8, NF), 1)
    return sub == lane % F8


def transform_chunk(first, load, centre, thi_ref, tlo_ref, w_ref, xhi, xlo, spec_ref, gram_ref, cols):
    for i in range(NB + 1):
        rows = slice(i * HALF, (i + 1) * HALF)
        xhi[rows], xlo[rows] = split(load(i) - centre)

    def one_window(b, _):
        rows = pl.ds(pl.multiple_of(b * HALF, HALF), NFFT)
        value = dot3((thi_ref[...], tlo_ref[...]), (xhi[rows], xlo[rows]))
        for ri in range(2):
            spec_ref[:, pl.ds(pl.multiple_of(ri * NF + b * F8, F8), F8), cols] = value[
                ri * NF : (ri + 1) * NF
            ].reshape(GROUPS, F8, -1)
        return 0

    lax.fori_loop(0, NB, one_window, 0, unroll=2)
    keep = same_frequency()[None]

    def one_group(g, _):
        parts = split(spec_ref[g, :, cols] * w_ref[:, cols])
        full = dot3(parts, parts, (((1,), (1,)), ((), ())))
        real = full[:NF, :NF] + full[NF:, NF:]
        imag = full[:NF, NF:] - full[NF:, :NF]
        for ri, value in enumerate((real, imag)):
            value = jnp.where(keep, value.reshape(NB, F8, NF), 0.0).sum(axis=1)
            rows = pl.ds(pl.multiple_of((ri * GROUPS + g) * NB, NB), NB)
            gram_ref[rows] = value if first else gram_ref[rows] + value
        return 0

    lax.fori_loop(0, GROUPS, one_group, 0, unroll=2)


def transform_kernel(width, x_ref, w_ref, thi_ref, tlo_ref, spec_ref, gram_ref, xhi, xlo):
    cells = x_ref.shape[1]
    for at in range(0, cells, width):
        cols = slice(at, at + width)
        centre = jnp.mean(x_ref[:, cols], axis=0, keepdims=True)
        transform_chunk(
            at == 0, lambda i: x_ref[i * HALF : (i + 1) * HALF, cols], centre,
            thi_ref, tlo_ref, w_ref, xhi, xlo, spec_ref, gram_ref, cols,
        )


def transform(series, weight):
    slices, cells = series.shape
    width = min(cells, 256)
    vmem = pl.BlockSpec(memory_space=pltpu.VMEM)
    return pl.pallas_call(
        functools.partial(transform_kernel, width),
        out_shape=(
            jax.ShapeDtypeStruct((GROUPS, 2 * NF, cells), F32),
            jax.ShapeDtypeStruct((2 * GROUPS * NB, NF), F32),
        ),
        in_specs=[vmem] * 4,
        out_specs=(vmem, vmem),
        scratch_shapes=[pltpu.VMEM((slices, width), BF16)] * 2,
        compiler_params=pltpu.CompilerParams(vmem_limit_bytes=48 * 2**20),
    )(series, weight, *window_table())


def peer(members, off):
    return {"cells": lax.rem(lax.axis_index("cells") + off, members)}


def greet(members):
    barrier = pltpu.get_barrier_semaphore()

    def one(off, _):
        pl.semaphore_signal(
            barrier, inc=1, device_id=peer(members, off), device_id_type=pl.DeviceIdType.MESH
        )
        return 0

    lax.fori_loop(1, members, one, 0)
    pl.semaphore_wait(barrier, members - 1)


def all_sum(members, part_ref, land, gather, sems):
    me = lax.axis_index("cells")
    rows = part_ref.shape[0] // members

    def of(member):
        return pl.ds(pl.multiple_of(member * rows, rows), rows)

    def share(off):
        return pltpu.make_async_remote_copy(
            src_ref=part_ref.at[of(lax.rem(me + off, members))],
            dst_ref=land.at[off],
            send_sem=sems.at[0, off],
            recv_sem=sems.at[1, off],
            device_id=peer(members, off),
            device_id_type=pl.DeviceIdType.MESH,
        )

    def result(off):
        return pltpu.make_async_remote_copy(
            src_ref=gather.at[of(me)],
            dst_ref=gather.at[of(me)],
            send_sem=sems.at[2, off],
            recv_sem=sems.at[3, off],
            device_id=peer(members, off),
            device_id_type=pl.DeviceIdType.MESH,
        )

    def loop(body):
        def one(off, _):
            body(off)
            return 0

        lax.fori_loop(1, members, one, 0)

    loop(lambda off: share(off).start())
    land[0] = part_ref[of(me)]
    loop(lambda off: share(off).wait())
    gather[of(me)] = jnp.sum(land[...], axis=0)
    loop(lambda off: result(off).start())
    loop(lambda off: result(off).wait())


def sum_kernel(members, part_ref, out_ref, land, gather, sems):
    greet(members)
    all_sum(members, part_ref, land, gather, sems)
    out_ref[...] = gather[...]


def sum_over_cells(gram, members):
    vmem = pl.BlockSpec(memory_space=pltpu.VMEM)
    return pl.pallas_call(
        functools.partial(sum_kernel, members),
        out_shape=jax.ShapeDtypeStruct(gram.shape, F32),
        in_specs=[vmem],
        out_specs=vmem,
        scratch_shapes=[
            pltpu.VMEM((members, gram.shape[0] // members, NF), F32),
            pltpu.VMEM(gram.shape, F32),
            pltpu.SemaphoreType.DMA((4, members)),
        ],
        compiler_params=pltpu.CompilerParams(collective_id=0, has_side_effects=True),
    )(gram)


def exchange_kernel(
    members, width, x_ref, w_ref, thi_ref, tlo_ref, spec_out, gram_out,
    arrived, spec, xhi, xlo, gram, land, gather, own_sem, send_sem, recv_sem, out_sem, sum_sem,
):
    me = lax.axis_index("cells")
    slices = x_ref.shape[0]
    cells = x_ref.shape[1] // members
    chunks = cells // width
    mine = pl.ds(pl.multiple_of(me * slices, 8), slices)

    def source(member, chunk):
        return x_ref.at[:, pl.ds(pl.multiple_of(member * cells + chunk * width, width), width)]

    def own(chunk):
        return pltpu.make_async_copy(
            source(me, chunk), arrived.at[chunk, mine], own_sem.at[chunk]
        )

    def remote(chunk, off):
        return pltpu.make_async_remote_copy(
            src_ref=source(lax.rem(me + off, members), chunk),
            dst_ref=arrived.at[chunk, mine],
            send_sem=send_sem.at[chunk, off],
            recv_sem=recv_sem.at[chunk, off],
            device_id=peer(members, off),
            device_id_type=pl.DeviceIdType.MESH,
        )

    def store(chunk):
        cols = slice(chunk * width, (chunk + 1) * width)
        return pltpu.make_async_copy(
            spec.at[:, :, cols], spec_out.at[:, :, cols], out_sem.at[chunk]
        )

    def loop(body):
        def one(off, _):
            body(off)
            return 0

        lax.fori_loop(1, members, one, 0)

    for chunk in range(chunks):
        own(chunk).start()
    greet(members)
    for chunk in range(chunks):
        for off in sorted(range(1, members), key=lambda off: abs(off - members // 2)):
            remote(chunk, off).start()
    for chunk in range(chunks):
        own(chunk).wait()
        loop(lambda off: remote(chunk, off).wait_recv())
        cols = slice(chunk * width, (chunk + 1) * width)
        centre = jnp.mean(arrived[chunk], axis=0, keepdims=True)
        transform_chunk(
            chunk == 0, lambda i: arrived[chunk, i * HALF : (i + 1) * HALF], centre,
            thi_ref, tlo_ref, w_ref, xhi, xlo, spec, gram, cols,
        )
        store(chunk).start()
    all_sum(members, gram, land, gather, sum_sem)
    gram_out[...] = gather[...]
    for chunk in range(chunks):
        loop(lambda off: remote(chunk, off).wait_send())
        store(chunk).wait()


def exchange(snapshots, weight, members):
    slices = snapshots.shape[0]
    cells = weight.shape[1]
    width = min(cells, WIDTH)
    chunks = cells // width
    total = slices * members
    spec = (GROUPS, 2 * NF, cells)
    gram = (2 * GROUPS * NB, NF)
    vmem = pl.BlockSpec(memory_space=pltpu.VMEM)
    anywhere = pl.BlockSpec(memory_space=pl.ANY)
    return pl.pallas_call(
        functools.partial(exchange_kernel, members, width),
        out_shape=(jax.ShapeDtypeStruct(spec, F32), jax.ShapeDtypeStruct(gram, F32)),
        in_specs=[anywhere, vmem, vmem, vmem],
        out_specs=(anywhere, vmem),
        scratch_shapes=[
            pltpu.VMEM((chunks, total, width), F32),
            pltpu.VMEM(spec, F32),
            pltpu.VMEM((total, width), BF16),
            pltpu.VMEM((total, width), BF16),
            pltpu.VMEM(gram, F32),
            pltpu.VMEM((members, gram[0] // members, NF), F32),
            pltpu.VMEM(gram, F32),
            pltpu.SemaphoreType.DMA((chunks,)),
            pltpu.SemaphoreType.DMA((chunks, members)),
            pltpu.SemaphoreType.DMA((chunks, members)),
            pltpu.SemaphoreType.DMA((chunks,)),
            pltpu.SemaphoreType.DMA((4, members)),
        ],
        compiler_params=pltpu.CompilerParams(
            collective_id=1, has_side_effects=True, vmem_limit_bytes=48 * 2**20
        ),
    )(snapshots, weight, *window_table())


def factor(gram_re, gram_im):
    shape = gram_re.shape
    row = lax.broadcasted_iota(jnp.int32, shape, 1)
    lane = lax.broadcasted_iota(jnp.int32, shape, 2)
    block = lane // F8
    flat = (shape[0] * shape[1], shape[2])
    lane2 = lax.broadcasted_iota(jnp.int32, flat, 1)
    a_re, a_im = gram_re, gram_im
    w_re = (row == block).astype(F32)
    w_im = jnp.zeros(shape, F32)
    for j in range(NB):
        index = j * F8 + lane2 % F8

        def spread(value):
            return jnp.take_along_axis(
                value.reshape(flat), index, axis=1, mode="promise_in_bounds"
            ).reshape(shape)

        c_re, c_im = spread(a_re), spread(a_im)
        inverse = 1.0 / jnp.sqrt(c_re[:, j : j + 1])
        l_re = jnp.where(row > j, c_re * inverse, 0.0)
        l_im = jnp.where(row > j, c_im * inverse, 0.0)

        def eliminate(v_re, v_im):
            p_re, p_im = v_re[:, j : j + 1] * inverse, v_im[:, j : j + 1] * inverse
            return (
                jnp.where(row == j, p_re, v_re - (l_re * p_re - l_im * p_im)),
                jnp.where(row == j, p_im, v_im - (l_re * p_im + l_im * p_re)),
            )

        a_re, a_im = eliminate(a_re, a_im)
        w_re, w_im = eliminate(w_re, w_im)
    a_re = jnp.where(block >= row, a_re, 0.0)
    a_im = jnp.where(block > row, a_im, 0.0)
    return a_re, a_im, w_re, w_im


def by_frequency(upper, out_ref, ri):
    block = lax.broadcasted_iota(jnp.int32, (NB, NF), 1) // F8
    turned = [pltpu.roll(upper[g], g * F8, 1) if g else upper[g] for g in range(GROUPS)]
    for k in range(NB):
        value = turned[0]
        for g in range(1, GROUPS):
            value = jnp.where(block == (g + k) % NB, turned[g], value)
        out_ref[ri, :, k, :] = pltpu.roll(value, (NF - k * F8) % NF, 1) if k else value


def modes_kernel(gram_ref, spec_ref, modes_ref, upper_ref, inv):
    @pl.when(pl.program_id(0) == 0)
    def _():
        upper_re, upper_im, inv[0], inv[1] = factor(gram_ref[0], gram_ref[1])
        for ri, upper in enumerate((upper_re, upper_im)):
            by_frequency(upper, upper_ref, ri)

    g = pl.program_id(0)
    sub = lax.broadcasted_iota(jnp.int32, (F8, NB, NF), 0)
    lane = lax.broadcasted_iota(jnp.int32, (F8, NB, NF), 2)
    keep = sub == lane % F8
    real, imag = [
        jnp.where(keep, jnp.broadcast_to(inv[ri, g][None], keep.shape), 0.0).reshape(NF, NF)
        for ri in range(2)
    ]
    matrix = jnp.concatenate(
        [jnp.concatenate([real, imag], axis=1), jnp.concatenate([-imag, real], axis=1)], axis=0
    )
    value = dot3(split(matrix), split(spec_ref[0]))
    modes_ref[...] = value.reshape(2, F8, NB, -1)


def finish(gram, spec):
    cells = spec.shape[2]
    whole = (2, GROUPS, NB, NF)
    return pl.pallas_call(
        modes_kernel,
        grid=(GROUPS,),
        out_shape=(
            jax.ShapeDtypeStruct((2, NF, NB, cells), F32),
            jax.ShapeDtypeStruct((2, NB, NB, NF), F32),
        ),
        in_specs=[
            pl.BlockSpec(whole, lambda g: (0, 0, 0, 0)),
            pl.BlockSpec((1, 2 * NF, cells), lambda g: (g, 0, 0)),
        ],
        out_specs=(
            pl.BlockSpec((2, F8, NB, cells), lambda g: (0, g, 0, 0)),
            pl.BlockSpec((2, NB, NB, NF), lambda g: (0, 0, 0, 0)),
        ),
        scratch_shapes=[pltpu.VMEM(whole, F32)],
        compiler_params=pltpu.CompilerParams(vmem_limit_bytes=56 * 2**20),
    )(gram, spec)


def on_device(snapshots, cell_volume):
    cells = cell_volume.shape[0]
    slices = snapshots.shape[0]
    members = lax.axis_size("cells")
    weight = jnp.sqrt(cell_volume / (cells * members))[None]
    if slices % 8 == 0 and cells % WIDTH == 0:
        spec, gram = exchange(snapshots, weight, members)
    else:
        blocks = snapshots.reshape(slices, members, cells)
        series = lax.all_to_all(blocks, "cells", split_axis=1, concat_axis=0, tiled=True)[:, 0, :]
        spec, gram = transform(series, weight)
        gram = sum_over_cells(gram, members)
    return finish(gram.reshape(2, GROUPS, NB, NF), spec)


def solution(mesh):
    return jax.shard_map(
        on_device,
        mesh=mesh,
        in_specs=(P("cells", "groups"), P(("groups", "cells"))),
        out_specs=(P(None, None, None, ("groups", "cells")), P("groups", None, None, None)),
        check_vma=False,
    )
```

```python
import functools

import jax
import jax.numpy as jnp
import ml_dtypes
import numpy as np
from jax import lax
from jax.experimental import pallas as pl
from jax.experimental.pallas import tpu as pltpu
from jax.sharding import PartitionSpec as P

NFFT = 256
NF = 128
NB = 16
HALF = NFFT // 2
F8 = 8
GROUPS = NF // F8
WIDTH = 128
BF16 = jnp.bfloat16
F32 = jnp.float32


def window_table():
    steps = np.arange(NFFT)
    freqs = np.arange(NF)
    window = 0.5 - 0.5 * np.cos(2.0 * np.pi * steps / NFFT)
    scale = 1.0 / np.sqrt(NB * np.sum(window * window))
    angle = 2.0 * np.pi * (freqs[:, None] * steps[None, :] % NFFT) / NFFT
    cosine = window[None, :] * np.cos(angle) * scale
    sine = -window[None, :] * np.sin(angle) * scale
    table = np.concatenate([cosine, sine], axis=0).astype(np.float32)
    high = table.astype(ml_dtypes.bfloat16)
    low = (table - high.astype(np.float32)).astype(ml_dtypes.bfloat16)
    return high, low


def split(value):
    high = value.astype(BF16)
    return high, (value - high.astype(F32)).astype(BF16)


def dot3(left, right, dims=(((1,), (0,)), ((), ()))):
    dot = functools.partial(lax.dot_general, dimension_numbers=dims, preferred_element_type=F32)
    return dot(left[0], right[0]) + (dot(left[0], right[1]) + dot(left[1], right[0]))


def same_frequency():
    sub = lax.broadcasted_iota(jnp.int32, (F8, NF), 0)
    lane = lax.broadcasted_iota(jnp.int32, (F8, NF), 1)
    return sub == lane % F8


def transform_chunk(first, load, centre, thi_ref, tlo_ref, w_ref, xhi, xlo, spec_ref, gram_ref, cols):
    for i in range(NB + 1):
        rows = slice(i * HALF, (i + 1) * HALF)
        xhi[rows], xlo[rows] = split(load(i) - centre)

    def one_window(b, _):
        rows = pl.ds(pl.multiple_of(b * HALF, HALF), NFFT)
        value = dot3((thi_ref[...], tlo_ref[...]), (xhi[rows], xlo[rows]))
        for ri in range(2):
            spec_ref[:, pl.ds(pl.multiple_of(ri * NF + b * F8, F8), F8), cols] = value[
                ri * NF : (ri + 1) * NF
            ].reshape(GROUPS, F8, -1)
        return 0

    lax.fori_loop(0, NB, one_window, 0, unroll=2)
    keep = same_frequency()[None]

    def one_group(g, _):
        parts = split(spec_ref[g, :, cols] * w_ref[:, cols])
        full = dot3(parts, parts, (((1,), (1,)), ((), ())))
        real = full[:NF, :NF] + full[NF:, NF:]
        imag = full[:NF, NF:] - full[NF:, :NF]
        for ri, value in enumerate((real, imag)):
            value = jnp.where(keep, value.reshape(NB, F8, NF), 0.0).sum(axis=1)
            rows = pl.ds(pl.multiple_of((ri * GROUPS + g) * NB, NB), NB)
            gram_ref[rows] = value if first else gram_ref[rows] + value
        return 0

    lax.fori_loop(0, GROUPS, one_group, 0, unroll=2)


def transform_kernel(width, x_ref, w_ref, thi_ref, tlo_ref, spec_ref, gram_ref, xhi, xlo):
    cells = x_ref.shape[1]
    for at in range(0, cells, width):
        cols = slice(at, at + width)
        centre = jnp.mean(x_ref[:, cols], axis=0, keepdims=True)
        transform_chunk(
            at == 0, lambda i: x_ref[i * HALF : (i + 1) * HALF, cols], centre,
            thi_ref, tlo_ref, w_ref, xhi, xlo, spec_ref, gram_ref, cols,
        )


def transform(series, weight):
    slices, cells = series.shape
    width = min(cells, 256)
    vmem = pl.BlockSpec(memory_space=pltpu.VMEM)
    return pl.pallas_call(
        functools.partial(transform_kernel, width),
        out_shape=(
            jax.ShapeDtypeStruct((GROUPS, 2 * NF, cells), F32),
            jax.ShapeDtypeStruct((2 * GROUPS * NB, NF), F32),
        ),
        in_specs=[vmem] * 4,
        out_specs=(vmem, vmem),
        scratch_shapes=[pltpu.VMEM((slices, width), BF16)] * 2,
        compiler_params=pltpu.CompilerParams(vmem_limit_bytes=48 * 2**20),
    )(series, weight, *window_table())


def peer(members, off):
    return {"cells": lax.rem(lax.axis_index("cells") + off, members)}


def greet(members):
    barrier = pltpu.get_barrier_semaphore()

    def one(off, _):
        pl.semaphore_signal(
            barrier, inc=1, device_id=peer(members, off), device_id_type=pl.DeviceIdType.MESH
        )
        return 0

    lax.fori_loop(1, members, one, 0)
    pl.semaphore_wait(barrier, members - 1)


def all_sum(members, part_ref, land, gather, sems):
    me = lax.axis_index("cells")
    rows = part_ref.shape[0] // members

    def of(member):
        return pl.ds(pl.multiple_of(member * rows, rows), rows)

    def share(off):
        return pltpu.make_async_remote_copy(
            src_ref=part_ref.at[of(lax.rem(me + off, members))],
            dst_ref=land.at[off],
            send_sem=sems.at[0, off],
            recv_sem=sems.at[1, off],
            device_id=peer(members, off),
            device_id_type=pl.DeviceIdType.MESH,
        )

    def result(off):
        return pltpu.make_async_remote_copy(
            src_ref=gather.at[of(me)],
            dst_ref=gather.at[of(me)],
            send_sem=sems.at[2, off],
            recv_sem=sems.at[3, off],
            device_id=peer(members, off),
            device_id_type=pl.DeviceIdType.MESH,
        )

    def loop(body):
        def one(off, _):
            body(off)
            return 0

        lax.fori_loop(1, members, one, 0)

    loop(lambda off: share(off).start())
    land[0] = part_ref[of(me)]
    loop(lambda off: share(off).wait())
    gather[of(me)] = jnp.sum(land[...], axis=0)
    loop(lambda off: result(off).start())
    loop(lambda off: result(off).wait())


def sum_kernel(members, part_ref, out_ref, land, gather, sems):
    greet(members)
    all_sum(members, part_ref, land, gather, sems)
    out_ref[...] = gather[...]


def sum_over_cells(gram, members):
    vmem = pl.BlockSpec(memory_space=pltpu.VMEM)
    return pl.pallas_call(
        functools.partial(sum_kernel, members),
        out_shape=jax.ShapeDtypeStruct(gram.shape, F32),
        in_specs=[vmem],
        out_specs=vmem,
        scratch_shapes=[
            pltpu.VMEM((members, gram.shape[0] // members, NF), F32),
            pltpu.VMEM(gram.shape, F32),
            pltpu.SemaphoreType.DMA((4, members)),
        ],
        compiler_params=pltpu.CompilerParams(collective_id=0, has_side_effects=True),
    )(gram)


def exchange_kernel(
    members, width, x_ref, w_ref, thi_ref, tlo_ref, spec_out, gram_out,
    arrived, spec, xhi, xlo, gram, land, gather, own_sem, send_sem, recv_sem, out_sem, sum_sem,
):
    me = lax.axis_index("cells")
    slices = x_ref.shape[0]
    cells = x_ref.shape[1] // members
    chunks = cells // width
    mine = pl.ds(pl.multiple_of(me * slices, 8), slices)

    def source(member, chunk):
        return x_ref.at[:, pl.ds(pl.multiple_of(member * cells + chunk * width, width), width)]

    def own(chunk):
        return pltpu.make_async_copy(
            source(me, chunk), arrived.at[chunk, mine], own_sem.at[chunk]
        )

    def remote(chunk, off):
        return pltpu.make_async_remote_copy(
            src_ref=source(lax.rem(me + off, members), chunk),
            dst_ref=arrived.at[chunk, mine],
            send_sem=send_sem.at[chunk, off],
            recv_sem=recv_sem.at[chunk, off],
            device_id=peer(members, off),
            device_id_type=pl.DeviceIdType.MESH,
        )

    def store(chunk):
        cols = slice(chunk * width, (chunk + 1) * width)
        return pltpu.make_async_copy(
            spec.at[:, :, cols], spec_out.at[:, :, cols], out_sem.at[chunk]
        )

    def loop(body):
        def one(off, _):
            body(off)
            return 0

        lax.fori_loop(1, members, one, 0)

    for chunk in range(chunks):
        own(chunk).start()
    greet(members)
    for chunk in range(chunks):
        for off in sorted(range(1, members), key=lambda off: abs(off - members // 2)):
            remote(chunk, off).start()
    for chunk in range(chunks):
        own(chunk).wait()
        loop(lambda off: remote(chunk, off).wait_recv())
        cols = slice(chunk * width, (chunk + 1) * width)
        centre = jnp.mean(arrived[chunk], axis=0, keepdims=True)
        transform_chunk(
            chunk == 0, lambda i: arrived[chunk, i * HALF : (i + 1) * HALF], centre,
            thi_ref, tlo_ref, w_ref, xhi, xlo, spec, gram, cols,
        )
        store(chunk).start()
    all_sum(members, gram, land, gather, sum_sem)
    gram_out[...] = gather[...]
    for chunk in range(chunks):
        loop(lambda off: remote(chunk, off).wait_send())
        store(chunk).wait()


def exchange(snapshots, weight, members):
    slices = snapshots.shape[0]
    cells = weight.shape[1]
    width = min(cells, WIDTH)
    chunks = cells // width
    total = slices * members
    spec = (GROUPS, 2 * NF, cells)
    gram = (2 * GROUPS * NB, NF)
    vmem = pl.BlockSpec(memory_space=pltpu.VMEM)
    anywhere = pl.BlockSpec(memory_space=pl.ANY)
    return pl.pallas_call(
        functools.partial(exchange_kernel, members, width),
        out_shape=(jax.ShapeDtypeStruct(spec, F32), jax.ShapeDtypeStruct(gram, F32)),
        in_specs=[anywhere, vmem, vmem, vmem],
        out_specs=(anywhere, vmem),
        scratch_shapes=[
            pltpu.VMEM((chunks, total, width), F32),
            pltpu.VMEM(spec, F32),
            pltpu.VMEM((total, width), BF16),
            pltpu.VMEM((total, width), BF16),
            pltpu.VMEM(gram, F32),
            pltpu.VMEM((members, gram[0] // members, NF), F32),
            pltpu.VMEM(gram, F32),
            pltpu.SemaphoreType.DMA((chunks,)),
            pltpu.SemaphoreType.DMA((chunks, members)),
            pltpu.SemaphoreType.DMA((chunks, members)),
            pltpu.SemaphoreType.DMA((chunks,)),
            pltpu.SemaphoreType.DMA((4, members)),
        ],
        compiler_params=pltpu.CompilerParams(
            collective_id=1, has_side_effects=True, vmem_limit_bytes=48 * 2**20
        ),
    )(snapshots, weight, *window_table())


def factor(gram_re, gram_im):
    shape = gram_re.shape
    row = lax.broadcasted_iota(jnp.int32, shape, 1)
    lane = lax.broadcasted_iota(jnp.int32, shape, 2)
    block = lane // F8
    flat = (shape[0] * shape[1], shape[2])
    lane2 = lax.broadcasted_iota(jnp.int32, flat, 1)
    a_re, a_im = gram_re, gram_im
    w_re = (row == block).astype(F32)
    w_im = jnp.zeros(shape, F32)
    for j in range(NB):
        index = j * F8 + lane2 % F8

        def spread(value):
            return jnp.take_along_axis(
                value.reshape(flat), index, axis=1, mode="promise_in_bounds"
            ).reshape(shape)

        c_re, c_im = spread(a_re), spread(a_im)
        inverse = 1.0 / jnp.sqrt(c_re[:, j : j + 1])
        l_re = jnp.where(row > j, c_re * inverse, 0.0)
        l_im = jnp.where(row > j, c_im * inverse, 0.0)

        def eliminate(v_re, v_im):
            p_re, p_im = v_re[:, j : j + 1] * inverse, v_im[:, j : j + 1] * inverse
            return (
                jnp.where(row == j, p_re, v_re - (l_re * p_re - l_im * p_im)),
                jnp.where(row == j, p_im, v_im - (l_re * p_im + l_im * p_re)),
            )

        a_re, a_im = eliminate(a_re, a_im)
        w_re, w_im = eliminate(w_re, w_im)
    a_re = jnp.where(block >= row, a_re, 0.0)
    a_im = jnp.where(block > row, a_im, 0.0)
    return a_re, a_im, w_re, w_im


def by_frequency(upper, out_ref, ri):
    block = lax.broadcasted_iota(jnp.int32, (NB, NF), 1) // F8
    turned = [pltpu.roll(upper[g], g * F8, 1) if g else upper[g] for g in range(GROUPS)]
    for k in range(NB):
        value = turned[0]
        for g in range(1, GROUPS):
            value = jnp.where(block == (g + k) % NB, turned[g], value)
        out_ref[ri, :, k, :] = pltpu.roll(value, (NF - k * F8) % NF, 1) if k else value


def modes_kernel(gram_ref, spec_ref, modes_ref, upper_ref, inv):
    @pl.when(pl.program_id(0) == 0)
    def _():
        upper_re, upper_im, inv[0], inv[1] = factor(gram_ref[0], gram_ref[1])
        for ri, upper in enumerate((upper_re, upper_im)):
            by_frequency(upper, upper_ref, ri)

    g = pl.program_id(0)
    sub = lax.broadcasted_iota(jnp.int32, (F8, NB, NF), 0)
    lane = lax.broadcasted_iota(jnp.int32, (F8, NB, NF), 2)
    keep = sub == lane % F8
    real, imag = [
        jnp.where(keep, jnp.broadcast_to(inv[ri, g][None], keep.shape), 0.0).reshape(NF, NF)
        for ri in range(2)
    ]
    matrix = jnp.concatenate(
        [jnp.concatenate([real, imag], axis=1), jnp.concatenate([-imag, real], axis=1)], axis=0
    )
    value = dot3(split(matrix), split(spec_ref[0]))
    modes_ref[...] = value.reshape(2, F8, NB, -1)


def finish(gram, spec):
    cells = spec.shape[2]
    whole = (2, GROUPS, NB, NF)
    return pl.pallas_call(
        modes_kernel,
        grid=(GROUPS,),
        out_shape=(
            jax.ShapeDtypeStruct((2, NF, NB, cells), F32),
            jax.ShapeDtypeStruct((2, NB, NB, NF), F32),
        ),
        in_specs=[
            pl.BlockSpec(whole, lambda g: (0, 0, 0, 0)),
            pl.BlockSpec((1, 2 * NF, cells), lambda g: (g, 0, 0)),
        ],
        out_specs=(
            pl.BlockSpec((2, F8, NB, cells), lambda g: (0, g, 0, 0)),
            pl.BlockSpec((2, NB, NB, NF), lambda g: (0, 0, 0, 0)),
        ),
        scratch_shapes=[pltpu.VMEM(whole, F32)],
        compiler_params=pltpu.CompilerParams(vmem_limit_bytes=32 * 2**20),
    )(gram, spec)


def on_device(snapshots, cell_volume):
    cells = cell_volume.shape[0]
    slices = snapshots.shape[0]
    members = lax.axis_size("cells")
    weight = jnp.sqrt(cell_volume / (cells * members))[None]
    if slices % 8 == 0 and cells % WIDTH == 0:
        spec, gram = exchange(snapshots, weight, members)
    else:
        blocks = snapshots.reshape(slices, members, cells)
        series = lax.all_to_all(blocks, "cells", split_axis=1, concat_axis=0, tiled=True)[:, 0, :]
        spec, gram = transform(series, weight)
        gram = sum_over_cells(gram, members)
    return finish(gram.reshape(2, GROUPS, NB, NF), spec)


def solution(mesh):
    return jax.shard_map(
        on_device,
        mesh=mesh,
        in_specs=(P("cells", "groups"), P(("groups", "cells"))),
        out_specs=(P(None, None, None, ("groups", "cells")), P("groups", None, None, None)),
        check_vma=False,
    )
```
